32 devices in a mesh: groups: 2 (over y), ctx: 8 (over z, x), head: 2 (over core).
Axes of the slice: x: 2, y: 2, z: 4, core: 2. Of those that a mesh axis runs over, the one named last changes fastest.
Arguments:
- hist_x: bfloat16 [4096, 1024], P(('groups', 'ctx')), parts along dimension 0, may hold values from -6 to 6
- cand_x: bfloat16 [64, 1024], P(('groups', 'ctx')), parts along dimension 0, may hold values from -6 to 6
- w_qkv: bfloat16 [3, 1024, 1024], P(None, None, 'head'), may hold values from -0.1875 to 0.1875
- rab_table: float32 [128, 8], P(None, 'head'), may hold values from -2 to 2
- hist_len: int32 [16], P(('groups', 'ctx')), parts along dimension 0, may hold values from 64 to 256, as said below
- hist_bucket: int32 [4096], P(('groups', 'ctx')), parts along dimension 0, may hold values from 0 to 127
- cand_owner: int32 [64], P('groups'), parts along dimension 0, may hold values from 0 to 31, each once
Outputs:
- hist_out: bfloat16 [4096, 1024], P(('groups', 'ctx'), 'head'), parts along dimension 0
- cand_out: bfloat16 [64, 1024], P(('groups', 'ctx'), 'head'), parts along dimension 0
The draws below stay inside these ranges and needn't reach their ends.
There are 2 independent parts, one for each index of `groups`. The reference program is written for one: setup_inputs(seed, part) draws one part's arguments, and reference() takes and returns one part's arrays. A program takes and returns all parts, laid end to end along the dimension named above; an argument that names none is the same for every part. Nothing has to cross between parts.
Inputs may be any that keep to these rules, and one draw needn't show every extreme that they name: `hist_len`: every index of ctx holds at least a quarter of its 256 events valid, and one index is full in every draw. `cand_owner`: each of 0 to 31 appears once.
All inputs are finite; a program needn't handle non-finite values.
Results may differ from the reference program's by a relative error of at most 0.0085.
Values may be sent and summed in bfloat16 or wider, within the bound.
A program may use at most 64 MiB of HBM per device.

```python
import jax
import jax.numpy as jnp
from jax import lax

HEADS = 8
HEAD_DIM = 128
D = 1024
NB = 128
WINDOW = 256
H_DEV = 256
HIST = 2048
CANDS = 32
N_CTX = 8


def draw_hist_len(key, part):
    key_lengths, key_spot = jax.random.split(jax.random.fold_in(key, 11))
    lengths = jax.random.randint(key_lengths, (N_CTX,), max(H_DEV // 4, 1), H_DEV + 1)
    full_spot = jax.random.randint(key_spot, (), 0, N_CTX)
    return jnp.where(jnp.arange(N_CTX) == full_spot, H_DEV, lengths).astype(jnp.int32)


def touch_ends(entries, stream_key, smallest, largest):
    place = [jax.random.randint(jax.random.fold_in(stream_key, axis), (), 0, length) for axis, length in enumerate(entries.shape)]
    main_axis = entries.shape.index(max(entries.shape))
    next_to = place[:main_axis] + [(place[main_axis] + 1) % entries.shape[main_axis]] + place[main_axis + 1:]
    return entries.at[tuple(place)].set(smallest).at[tuple(next_to)].set(largest)


def block_levels(own_key, extent, cuts, least, largest):
    level = 1.0
    for dim, parts in cuts:
        steps = jax.random.uniform(jax.random.fold_in(jax.random.fold_in(own_key, 6), dim), (parts,), jnp.float32, least / len(cuts), largest / len(cuts))
        level = level * jnp.repeat(jnp.exp(steps), extent[dim] // parts).reshape((-1,) + (1,) * (len(extent) - 1 - dim))
    return level


def gaussian(rng, shape, scale, reach, cuts=(), held_as=jnp.bfloat16):
    values = jax.random.normal(rng, shape, jnp.float32) * scale
    if len(cuts) > 0:
        values = block_levels(rng, shape, cuts, -0.22, 0.18) * values
    return jnp.clip(values, min=-reach, max=reach).astype(held_as)


def setup_inputs(seed: int = 0, part: int = 0) -> dict:
    key_of = jax.random.split(jax.random.key(seed), 8)
    own_keys = jax.random.split(jax.random.fold_in(key_of[7], part), 8)
    return {
        "hist_x": gaussian(own_keys[0], (HIST, D), 1.0, 6.0, ((0, 8),)),
        "cand_x": gaussian(own_keys[1], (CANDS, D), 1.0, 6.0, ((0, 8),)),
        "w_qkv": gaussian(key_of[2], (3, D, D), D ** -0.5, 0.1875, ((2, 2),)),
        "rab_table": jnp.clip(jax.random.uniform(key_of[3], (NB, HEADS), jnp.float32, -2.0, 2.0) * block_levels(key_of[3], (NB, HEADS), ((1, 2),), -0.4, 0.0), -2.0, 2.0),
        "hist_len": draw_hist_len(jax.random.fold_in(jax.random.fold_in(key_of[7], part), 71), part),
        "hist_bucket": touch_ends(jax.random.randint(own_keys[5], (HIST,), 0, NB), jax.random.fold_in(own_keys[5], 1), 0, NB - 1).astype(jnp.int32),
        "cand_owner": jax.random.permutation(own_keys[6], CANDS).astype(jnp.int32),
    }


def reference(hist_x, cand_x, w_qkv, rab_table, hist_len, hist_bucket, cand_owner):
    score_scale = HEAD_DIM ** -0.5
    queries = jnp.dot(hist_x, w_qkv[0], preferred_element_type=jnp.float32).astype(jnp.bfloat16)
    key_rows = jnp.dot(hist_x, w_qkv[1], preferred_element_type=jnp.float32).astype(jnp.bfloat16)
    raw_values = jnp.dot(hist_x, w_qkv[2], preferred_element_type=jnp.float32).astype(jnp.bfloat16)
    position = jnp.arange(HIST, dtype=jnp.int32)
    is_valid = (position % H_DEV) < hist_len[position // H_DEV]
    values = jnp.where(is_valid[:, None], raw_values, jnp.zeros((), jnp.bfloat16))
    key_bias = rab_table[hist_bucket].T.astype(jnp.bfloat16)
    key_padded = jnp.concatenate([jnp.zeros((WINDOW, D), jnp.bfloat16), key_rows], 0)
    value_padded = jnp.concatenate([jnp.zeros((WINDOW, D), jnp.bfloat16), values], 0)
    bias_padded = jnp.concatenate([jnp.zeros((HEADS, WINDOW), jnp.bfloat16), key_bias], 1)
    distance = jnp.arange(WINDOW, dtype=jnp.int32)[:, None] + WINDOW - jnp.arange(2 * WINDOW, dtype=jnp.int32)[None, :]
    in_window = (distance >= 0) & (distance < WINDOW)

    def window_block(first_row):
        q_block = lax.dynamic_slice_in_dim(queries, first_row, WINDOW, 0).astype(jnp.float32).reshape(WINDOW, HEADS, HEAD_DIM)
        k_block = lax.dynamic_slice_in_dim(key_padded, first_row, 2 * WINDOW, 0).astype(jnp.float32).reshape(2 * WINDOW, HEADS, HEAD_DIM)
        v_block = lax.dynamic_slice_in_dim(value_padded, first_row, 2 * WINDOW, 0).astype(jnp.float32).reshape(2 * WINDOW, HEADS, HEAD_DIM)
        b_block = lax.dynamic_slice_in_dim(bias_padded, first_row, 2 * WINDOW, 1).astype(jnp.float32)
        scores = jnp.einsum('qhd,khd->hqk', q_block, k_block) * score_scale + b_block[:, None, :]
        weights = jnp.where(in_window[None], jax.nn.silu(scores), 0.0).astype(jnp.bfloat16)
        weights = lax.optimization_barrier(weights).astype(jnp.float32)
        return jnp.einsum('hqk,khd->qhd', weights, v_block).reshape(WINDOW, D)

    block_starts = jnp.arange(HIST // WINDOW, dtype=jnp.int32) * WINDOW
    hist_sum = lax.map(window_block, block_starts).reshape(HIST, D)
    hist_out = jnp.where(is_valid[:, None], hist_sum * (WINDOW ** -0.5), 0.0).astype(jnp.bfloat16)

    cand_query = jnp.dot(cand_x, w_qkv[0], preferred_element_type=jnp.float32).astype(jnp.bfloat16)
    cand_heads = cand_query.astype(jnp.float32).reshape(CANDS, HEADS, HEAD_DIM)

    def cand_block(carry, first_row):
        k_block = lax.dynamic_slice_in_dim(key_rows, first_row, WINDOW, 0).astype(jnp.float32).reshape(WINDOW, HEADS, HEAD_DIM)
        v_block = lax.dynamic_slice_in_dim(values, first_row, WINDOW, 0).astype(jnp.float32).reshape(WINDOW, HEADS, HEAD_DIM)
        b_block = lax.dynamic_slice_in_dim(key_bias, first_row, WINDOW, 1).astype(jnp.float32)
        scores = jnp.einsum('chd,khd->hck', cand_heads, k_block) * score_scale + b_block[:, None, :]
        weights = lax.optimization_barrier(jax.nn.silu(scores).astype(jnp.bfloat16)).astype(jnp.float32)
        return carry + jnp.einsum('hck,khd->chd', weights, v_block).reshape(CANDS, D), None

    cand_sum, unused_out = lax.scan(cand_block, jnp.zeros((CANDS, D), jnp.float32), block_starts)
    cand_sum = cand_sum * (HIST ** -0.5)
    cand_out = jnp.zeros((CANDS, D), cand_sum.dtype).at[cand_owner].set(cand_sum).astype(jnp.bfloat16)
    return hist_out, cand_out
```

```python
import functools

import jax
import jax.numpy as jnp
from jax import lax
from jax.experimental import pallas as pl
from jax.experimental.pallas import tpu as pltpu
from jax.sharding import PartitionSpec as P

WINDOW = 256
CHUNKS = 2
MESH = pl.DeviceIdType.MESH
F32 = jnp.float32
BF16 = jnp.bfloat16


def dot(a, b):
    return jnp.dot(a, b, preferred_element_type=F32)


def dot_t(a, b):
    return lax.dot_general(a, b, (((1,), (1,)), ((), ())), preferred_element_type=F32)


def silu_from_half(t):
    return t + t * jnp.tanh(t)


def kernel(
    n,
    cores,
    heads,
    x_hbm,
    w_hbm,
    cand_ref,
    table_ref,
    len_ref,
    bucket_ref,
    owner_ref,
    out_ref,
    cand_out_ref,
    x_v,
    w_v,
    q_v,
    k_v,
    v_v,
    xe,
    ke_v,
    ve_v,
    acc,
    aux,
    aux_e,
    cand_rows,
    q_send,
    q_recv,
    p_send,
    p_recv,
    load_sem,
    qs_sem,
    qr_sem,
    ps_sem,
    pr_sem,
    es_sem,
    er_sem,
    as_sem,
    ar_sem,
    fs_sem,
    fr_sem,
):
    group = lax.axis_index("groups")
    me = lax.axis_index("ctx")
    core = lax.axis_index("head")
    rows, width = x_v.shape
    part = q_v.shape[1]
    size = part // heads
    half_scale = 0.5 * size ** (-0.5)
    cands = cand_ref.shape[0]
    total = cands * n
    slot = cands * heads
    fold = max(1, 8 // cands)
    unroll = n <= 16

    def peers(body):
        if unroll:
            for step in range(1, n):
                body(step)
        else:
            lax.fori_loop(1, n, lambda step, carry: (body(step), carry)[1], 0)

    loads = [pltpu.make_async_copy(w_hbm.at[0], w_v.at[0], load_sem.at[0])]
    loads.append(pltpu.make_async_copy(x_hbm, x_v, load_sem.at[3]))
    loads.append(pltpu.make_async_copy(w_hbm.at[1], w_v.at[1], load_sem.at[1]))
    loads.append(pltpu.make_async_copy(w_hbm.at[2], w_v.at[2], load_sem.at[2]))
    for load in loads:
        load.start()

    barrier = pltpu.get_barrier_semaphore()

    def greet(step):
        pl.semaphore_signal(
            barrier,
            inc=1,
            device_id=(group, lax.rem(me + step, n), core),
            device_id_type=MESH,
        )

    peers(greet)
    for step in range(1, cores):
        pl.semaphore_signal(
            barrier,
            inc=1,
            device_id=(group, me, lax.rem(core + step, cores)),
            device_id_type=MESH,
        )

    buckets = table_ref.shape[0]
    hot = (
        lax.broadcasted_iota(jnp.int32, (buckets, rows), 0) == bucket_ref[...]
    ).astype(F32)
    bias = lax.dot_general(
        table_ref[...].astype(BF16),
        hot.astype(BF16),
        (((0,), (0,)), ((), ())),
        preferred_element_type=F32,
    )
    aux[...] = jnp.full(aux.shape, len_ref[0].astype(F32), F32)
    aux[pl.ds(0, heads), :] = 0.5 * bias

    for head in range(heads):
        cand_rows[pl.ds(head * cands, cands), :] = cand_ref[...].astype(F32)
    loads[0].wait()
    own = dot(cand_rows[...].astype(BF16), w_v[0])
    row_head = lax.broadcasted_iota(jnp.int32, (slot, size), 0) // cands
    picked = own[:, 0:size]
    for head in range(1, heads):
        picked = jnp.where(row_head == head, own[:, head * size : (head + 1) * size], picked)
    q_send[...] = picked.astype(BF16)
    own_slot = pl.ds(pl.multiple_of(me * slot, slot), slot)
    q_recv[own_slot, :] = picked.astype(BF16)

    pl.semaphore_wait(barrier, n - 1 + cores - 1)

    def query_copy(step):
        return pltpu.make_async_remote_copy(
            src_ref=q_send,
            dst_ref=q_recv.at[own_slot, :],
            send_sem=qs_sem.at[step],
            recv_sem=qr_sem.at[step],
            device_id=(group, lax.rem(me + step, n), core),
            device_id_type=MESH,
        )

    peers(lambda step: query_copy(step).start())

    chunk = rows // (cores * CHUNKS)

    def rows_of(owner_core, index):
        first = owner_core * (chunk * CHUNKS) + index * chunk
        return pl.ds(pl.multiple_of(first, chunk), chunk)

    def edge_copy(index):
        return pltpu.make_async_remote_copy(
            src_ref=x_hbm.at[rows_of(core, index), :],
            dst_ref=xe.at[rows_of(core, index), :],
            send_sem=es_sem.at[index],
            recv_sem=er_sem.at[index],
            device_id=(group, lax.rem(me + 1, n), core),
            device_id_type=MESH,
        )

    aux_copy = pltpu.make_async_remote_copy(
        src_ref=aux,
        dst_ref=aux_e,
        send_sem=as_sem,
        recv_sem=ar_sem,
        device_id=(group, lax.rem(me + 1, n), core),
        device_id_type=MESH,
    )

    def forward(step, index):
        return pltpu.make_async_remote_copy(
            src_ref=xe.at[rows_of(core, index), :],
            dst_ref=xe.at[rows_of(core, index), :],
            send_sem=fs_sem.at[step - 1, index],
            recv_sem=fr_sem.at[step - 1, index],
            device_id=(group, me, lax.rem(core + step, cores)),
            device_id_type=MESH,
        )

    @pl.when(me < n - 1)
    def _():
        aux_copy.start()
        for index in range(CHUNKS):
            edge_copy(index).start()

    loads[1].wait()
    loads[2].wait()
    k_v[...] = dot(x_v[...], w_v[1]).astype(BF16)
    loads[3].wait()
    valid = lax.broadcasted_iota(jnp.int32, (rows, part), 0) < len_ref[0]
    v_v[...] = jnp.where(valid, dot(x_v[...], w_v[2]), 0.0).astype(BF16)

    group_heads = heads // fold
    out_rows = n * fold * cands
    tall = lax.broadcasted_iota(jnp.int32, (out_rows, total), 0)
    place = (tall // (fold * cands)) * cands + lax.rem(tall, cands)
    sits = (owner_ref[...] == place).astype(F32).astype(BF16)
    lane = lax.broadcasted_iota(jnp.int32, (total, n * slot), 1)
    source = (lane // slot) * cands + lax.rem(lane, cands)
    spread = (lax.broadcasted_iota(jnp.int32, (total, n * slot), 0) == source).astype(F32)
    chosen = dot(sits, spread.astype(BF16))
    lane_head = lax.rem(
        lax.broadcasted_iota(jnp.int32, (out_rows, n * slot), 1) // cands, heads
    )
    row_fold = lax.rem(
        lax.broadcasted_iota(jnp.int32, (out_rows, n * slot), 0) // cands, fold
    )
    peers(lambda step: query_copy(step).wait_recv())
    norm = (rows * n) ** (-0.5)

    def folded(parts, shape):
        fold_of = lax.rem(lax.broadcasted_iota(jnp.int32, shape, 0) // cands, fold)
        value = parts[0]
        for index in range(1, fold):
            value = jnp.where(fold_of == index, parts[index], value)
        return value

    for column in range(group_heads):
        select = jnp.where(lane_head == row_fold * group_heads + column, chosen, 0.0)
        query = dot(select.astype(BF16), q_recv[...]).astype(BF16)
        heads_here = [f * group_heads + column for f in range(fold)]
        spans = [slice(h * size, (h + 1) * size) for h in heads_here]
        t = folded(
            [
                dot_t(query, k_v[:, span]) * half_scale + aux[pl.ds(h, 1), :]
                for h, span in zip(heads_here, spans)
            ],
            (out_rows, rows),
        )
        weight = silu_from_half(t).astype(BF16)
        p_send[:, column * size : (column + 1) * size] = norm * folded(
            [dot(weight, v_v[:, span]) for span in spans], (out_rows, size)
        )
    tile = fold * cands
    own_tile = pl.ds(pl.multiple_of(me * tile, tile), tile)

    def partial_copy(step):
        to = lax.rem(me + step, n)
        return pltpu.make_async_remote_copy(
            src_ref=p_send.at[pl.ds(pl.multiple_of(to * tile, tile), tile), :],
            dst_ref=p_recv.at[own_tile, :],
            send_sem=ps_sem.at[step],
            recv_sem=pr_sem.at[step],
            device_id=(group, to, core),
            device_id_type=MESH,
        )

    peers(lambda step: partial_copy(step).start())
    p_recv[own_tile, :] = p_send[own_tile, :]

    q_v[...] = dot(x_v[...], w_v[0]).astype(BF16)
    below = lax.broadcasted_iota(jnp.int32, (rows, rows), 0) >= lax.broadcasted_iota(
        jnp.int32, (rows, rows), 1
    )
    for head in range(heads):
        span = slice(head * size, (head + 1) * size)
        t = dot_t(q_v[:, span], k_v[:, span]) * half_scale + aux[pl.ds(head, 1), :]
        weight = jnp.where(below, silu_from_half(t), 0.0).astype(BF16)
        acc[:, span] = dot(weight, v_v[:, span])

    out_scale = WINDOW ** (-0.5)

    @pl.when(me == 0)
    def _():
        out_ref[...] = jnp.where(valid, acc[...] * out_scale, 0.0).astype(BF16)

    @pl.when(me > 0)
    def _():
        for index in range(CHUNKS):
            edge_copy(index).wait_recv()
            for step in range(1, cores):
                forward(step, index).start()
        aux_copy.wait_recv()
        for step in range(1, cores):
            for index in range(CHUNKS):
                forward(step, index).wait_recv()
        ke_v[...] = dot(xe[...], w_v[1]).astype(BF16)
        edge_valid = (
            lax.broadcasted_iota(jnp.int32, (rows, part), 0).astype(F32) < aux_e[heads, 0]
        )
        ve_v[...] = jnp.where(edge_valid, dot(xe[...], w_v[2]), 0.0).astype(BF16)
        for head in range(heads):
            span = slice(head * size, (head + 1) * size)
            t = dot_t(q_v[:, span], ke_v[:, span]) * half_scale + aux_e[pl.ds(head, 1), :]
            weight = jnp.where(below, 0.0, silu_from_half(t)).astype(BF16)
            value = (acc[:, span] + dot(weight, ve_v[:, span])) * out_scale
            out_ref[:, span] = jnp.where(valid[:, span], value, 0.0).astype(BF16)
        for step in range(1, cores):
            for index in range(CHUNKS):
                forward(step, index).wait_send()

    peers(lambda step: partial_copy(step).wait_recv())
    if unroll:
        summed = p_recv[pl.ds(0, tile), :]
        for index in range(1, n):
            summed = summed + p_recv[pl.ds(index * tile, tile), :]
    else:
        summed = lax.fori_loop(
            0,
            n,
            lambda i, s: s + p_recv[pl.ds(pl.multiple_of(i * tile, tile), tile), :],
            jnp.zeros((tile, p_recv.shape[1]), F32),
        )
    group_width = group_heads * size
    for index in range(fold):
        cand_out_ref[:, index * group_width : (index + 1) * group_width] = summed[
            index * cands : (index + 1) * cands, :
        ].astype(BF16)

    peers(lambda step: query_copy(step).wait_send())
    peers(lambda step: partial_copy(step).wait_send())

    @pl.when(me < n - 1)
    def _():
        aux_copy.wait_send()
        for index in range(CHUNKS):
            edge_copy(index).wait_send()


def local(n, cores, hist_x, cand_x, w_qkv, rab_table, hist_len, hist_bucket, cand_owner):
    rows, width = hist_x.shape
    part = w_qkv.shape[2]
    heads = rab_table.shape[1]
    size = part // heads
    cands = cand_x.shape[0]
    slot = cands * heads
    fold = max(1, 8 // cands)
    tile = fold * cands
    dma = pltpu.SemaphoreType.DMA
    vmem = pl.BlockSpec(memory_space=pltpu.VMEM)
    hbm = pl.BlockSpec(memory_space=pltpu.HBM)
    smem = pl.BlockSpec(memory_space=pltpu.SMEM)
    return pl.pallas_call(
        functools.partial(kernel, n, cores, heads),
        out_shape=(
            jax.ShapeDtypeStruct((rows, part), BF16),
            jax.ShapeDtypeStruct((cands, part), BF16),
        ),
        in_specs=[hbm, hbm, vmem, vmem, smem, vmem, vmem],
        out_specs=(vmem, vmem),
        scratch_shapes=[
            pltpu.VMEM((rows, width), BF16),
            pltpu.VMEM(w_qkv.shape, BF16),
            pltpu.VMEM((rows, part), BF16),
            pltpu.VMEM((rows, part), BF16),
            pltpu.VMEM((rows, part), BF16),
            pltpu.VMEM((rows, width), BF16),
            pltpu.VMEM((rows, part), BF16),
            pltpu.VMEM((rows, part), BF16),
            pltpu.VMEM((rows, part), F32),
            pltpu.VMEM((8, rows), F32),
            pltpu.VMEM((8, rows), F32),
            pltpu.VMEM((slot, width), F32),
            pltpu.VMEM((slot, size), BF16),
            pltpu.VMEM((n * slot, size), BF16),
            pltpu.VMEM((n * tile, part // fold), F32),
            pltpu.VMEM((n * tile, part // fold), F32),
            dma((4,)),
            dma((n,)),
            dma((n,)),
            dma((n,)),
            dma((n,)),
            dma((CHUNKS,)),
            dma((CHUNKS,)),
            dma,
            dma,
            dma((max(cores - 1, 1), CHUNKS)),
            dma((max(cores - 1, 1), CHUNKS)),
        ],
        compiler_params=pltpu.CompilerParams(
            collective_id=0,
            has_side_effects=True,
            vmem_limit_bytes=48 * 1024 * 1024,
        ),
    )(
        hist_x,
        w_qkv,
        cand_x,
        rab_table,
        hist_len,
        hist_bucket.reshape(1, rows),
        cand_owner.reshape(1, cands * n),
    )


def solution(mesh):
    placed = (
        P(("groups", "ctx"), None),
        P(("groups", "ctx"), None),
        P(None, None, "head"),
        P(None, "head"),
        P(("groups", "ctx")),
        P(("groups", "ctx")),
        P("groups"),
    )
    return jax.shard_map(
        functools.partial(local, mesh.shape["ctx"], mesh.shape["head"]),
        mesh=mesh,
        in_specs=placed,
        out_specs=(P(("groups", "ctx"), "head"), P(("groups", "ctx"), "head")),
        check_vma=False,
    )
```

```python
import functools

import jax
import jax.numpy as jnp
from jax import lax
from jax.experimental import pallas as pl
from jax.experimental.pallas import tpu as pltpu
from jax.sharding import PartitionSpec as P

WINDOW = 256
CHUNKS = 2
VMEM_LIMIT = 63 * 1024 * 1024
MESH = pl.DeviceIdType.MESH
F32 = jnp.float32
BF16 = jnp.bfloat16


def dot(a, b):
    return jnp.dot(a, b, preferred_element_type=F32)


def dot_t(a, b):
    return lax.dot_general(a, b, (((1,), (1,)), ((), ())), preferred_element_type=F32)


def silu_from_half(t):
    return t + t * jnp.tanh(t)


def kernel(
    n,
    cores,
    heads,
    x_hbm,
    w_hbm,
    cand_hbm,
    table_hbm,
    len_hbm,
    bucket_hbm,
    owner_hbm,
    out_ref,
    cand_out_ref,
    cand_ref,
    table_ref,
    len_ref,
    bucket_ref,
    owner_ref,
    x_v,
    w_v,
    q_v,
    k_v,
    v_v,
    xe,
    ke_v,
    ve_v,
    acc,
    aux,
    aux_e,
    cand_rows,
    q_send,
    q_recv,
    p_send,
    p_recv,
    load_sem,
    qs_sem,
    qr_sem,
    ps_sem,
    pr_sem,
    es_sem,
    er_sem,
    as_sem,
    ar_sem,
    fs_sem,
    fr_sem,
):
    group = lax.axis_index("groups")
    me = lax.axis_index("ctx")
    core = lax.axis_index("head")
    rows, width = x_v.shape
    part = q_v.shape[1]
    size = part // heads
    half_scale = 0.5 * size ** (-0.5)
    cands = cand_ref.shape[0]
    total = cands * n
    slot = cands * heads
    fold = max(1, 8 // cands)
    unroll = n <= 16

    def peers(body):
        if unroll:
            for step in range(1, n):
                body(step)
        else:
            lax.fori_loop(1, n, lambda step, carry: (body(step), carry)[1], 0)

    pairs = [
        (cand_hbm, cand_ref),
        (len_hbm, len_ref),
        (bucket_hbm, bucket_ref),
        (table_hbm, table_ref),
        (owner_hbm, owner_ref),
        (w_hbm.at[0], w_v.at[0]),
        (x_hbm, x_v),
        (w_hbm.at[1], w_v.at[1]),
        (w_hbm.at[2], w_v.at[2]),
    ]
    loads = [
        pltpu.make_async_copy(source, target, load_sem.at[index])
        for index, (source, target) in enumerate(pairs)
    ]
    for load in loads:
        load.start()

    barrier = pltpu.get_barrier_semaphore()

    def greet(step):
        pl.semaphore_signal(
            barrier,
            inc=1,
            device_id=(group, lax.rem(me + step, n), core),
            device_id_type=MESH,
        )

    peers(greet)
    for step in range(1, cores):
        pl.semaphore_signal(
            barrier,
            inc=1,
            device_id=(group, me, lax.rem(core + step, cores)),
            device_id_type=MESH,
        )

    for load in loads[:5]:
        load.wait()

    buckets = table_ref.shape[1]
    hot = (
        lax.broadcasted_iota(jnp.int32, (buckets, rows), 0) == bucket_ref[...]
    ).astype(F32)
    bias = lax.dot_general(
        table_ref[...].astype(BF16),
        hot.astype(BF16),
        (((1,), (0,)), ((), ())),
        preferred_element_type=F32,
    )
    aux[...] = jnp.full(aux.shape, len_ref[0].astype(F32), F32)
    aux[pl.ds(0, heads), :] = 0.5 * bias

    for head in range(heads):
        cand_rows[pl.ds(head * cands, cands), :] = cand_ref[...].astype(F32)
    loads[5].wait()
    own = dot(cand_rows[...].astype(BF16), w_v[0])
    row_head = lax.broadcasted_iota(jnp.int32, (slot, size), 0) // cands
    picked = own[:, 0:size]
    for head in range(1, heads):
        picked = jnp.where(row_head == head, own[:, head * size : (head + 1) * size], picked)
    q_send[...] = picked.astype(BF16)
    own_slot = pl.ds(pl.multiple_of(me * slot, slot), slot)
    q_recv[own_slot, :] = picked.astype(BF16)

    pl.semaphore_wait(barrier, n - 1 + cores - 1)

    def query_copy(step):
        return pltpu.make_async_remote_copy(
            src_ref=q_send,
            dst_ref=q_recv.at[own_slot, :],
            send_sem=qs_sem.at[step],
            recv_sem=qr_sem.at[step],
            device_id=(group, lax.rem(me + step, n), core),
            device_id_type=MESH,
        )

    peers(lambda step: query_copy(step).start())

    chunk = rows // (cores * CHUNKS)

    def rows_of(owner_core, index):
        first = owner_core * (chunk * CHUNKS) + index * chunk
        return pl.ds(pl.multiple_of(first, chunk), chunk)

    def edge_copy(index):
        return pltpu.make_async_remote_copy(
            src_ref=x_hbm.at[rows_of(core, index), :],
            dst_ref=xe.at[rows_of(core, index), :],
            send_sem=es_sem.at[index],
            recv_sem=er_sem.at[index],
            device_id=(group, lax.rem(me + 1, n), core),
            device_id_type=MESH,
        )

    aux_copy = pltpu.make_async_remote_copy(
        src_ref=aux,
        dst_ref=aux_e,
        send_sem=as_sem,
        recv_sem=ar_sem,
        device_id=(group, lax.rem(me + 1, n), core),
        device_id_type=MESH,
    )

    def forward(step, index):
        return pltpu.make_async_remote_copy(
            src_ref=xe.at[rows_of(core, index), :],
            dst_ref=xe.at[rows_of(core, index), :],
            send_sem=fs_sem.at[step - 1, index],
            recv_sem=fr_sem.at[step - 1, index],
            device_id=(group, me, lax.rem(core + step, cores)),
            device_id_type=MESH,
        )

    @pl.when(me < n - 1)
    def _():
        aux_copy.start()
        for index in range(CHUNKS):
            edge_copy(index).start()

    loads[6].wait()
    loads[7].wait()
    k_v[...] = dot(x_v[...], w_v[1]).astype(BF16)
    loads[8].wait()
    valid = lax.broadcasted_iota(jnp.int32, (rows, part), 0) < len_ref[0]
    v_v[...] = jnp.where(valid, dot(x_v[...], w_v[2]), 0.0).astype(BF16)

    group_heads = heads // fold
    out_rows = n * fold * cands
    tall = lax.broadcasted_iota(jnp.int32, (out_rows, total), 0)
    place = (tall // (fold * cands)) * cands + lax.rem(tall, cands)
    sits = (owner_ref[...] == place).astype(F32).astype(BF16)
    lane = lax.broadcasted_iota(jnp.int32, (total, n * slot), 1)
    source = (lane // slot) * cands + lax.rem(lane, cands)
    spread = (lax.broadcasted_iota(jnp.int32, (total, n * slot), 0) == source).astype(F32)
    chosen = dot(sits, spread.astype(BF16))
    lane_head = lax.rem(
        lax.broadcasted_iota(jnp.int32, (out_rows, n * slot), 1) // cands, heads
    )
    row_fold = lax.rem(
        lax.broadcasted_iota(jnp.int32, (out_rows, n * slot), 0) // cands, fold
    )
    peers(lambda step: query_copy(step).wait_recv())
    norm = (rows * n) ** (-0.5)

    def folded(parts, shape):
        fold_of = lax.rem(lax.broadcasted_iota(jnp.int32, shape, 0) // cands, fold)
        value = parts[0]
        for index in range(1, fold):
            value = jnp.where(fold_of == index, parts[index], value)
        return value

    for column in range(group_heads):
        select = jnp.where(lane_head == row_fold * group_heads + column, chosen, 0.0)
        query = dot(select.astype(BF16), q_recv[...]).astype(BF16)
        heads_here = [f * group_heads + column for f in range(fold)]
        spans = [slice(h * size, (h + 1) * size) for h in heads_here]
        t = folded(
            [
                dot_t(query, k_v[:, span]) * half_scale + aux[pl.ds(h, 1), :]
                for h, span in zip(heads_here, spans)
            ],
            (out_rows, rows),
        )
        weight = silu_from_half(t).astype(BF16)
        p_send[:, column * size : (column + 1) * size] = norm * folded(
            [dot(weight, v_v[:, span]) for span in spans], (out_rows, size)
        )
    tile = fold * cands
    own_tile = pl.ds(pl.multiple_of(me * tile, tile), tile)

    def partial_copy(step):
        to = lax.rem(me + step, n)
        return pltpu.make_async_remote_copy(
            src_ref=p_send.at[pl.ds(pl.multiple_of(to * tile, tile), tile), :],
            dst_ref=p_recv.at[own_tile, :],
            send_sem=ps_sem.at[step],
            recv_sem=pr_sem.at[step],
            device_id=(group, to, core),
            device_id_type=MESH,
        )

    peers(lambda step: partial_copy(step).start())
    p_recv[own_tile, :] = p_send[own_tile, :]

    q_v[...] = dot(x_v[...], w_v[0]).astype(BF16)
    below = lax.broadcasted_iota(jnp.int32, (rows, rows), 0) >= lax.broadcasted_iota(
        jnp.int32, (rows, rows), 1
    )
    for head in range(heads):
        span = slice(head * size, (head + 1) * size)
        t = dot_t(q_v[:, span], k_v[:, span]) * half_scale + aux[pl.ds(head, 1), :]
        weight = jnp.where(below, silu_from_half(t), 0.0).astype(BF16)
        acc[:, span] = dot(weight, v_v[:, span])

    out_scale = WINDOW ** (-0.5)

    @pl.when(me == 0)
    def _():
        out_ref[...] = jnp.where(valid, acc[...] * out_scale, 0.0).astype(BF16)

    @pl.when(me > 0)
    def _():
        for index in range(CHUNKS):
            edge_copy(index).wait_recv()
            for step in range(1, cores):
                forward(step, index).start()
        aux_copy.wait_recv()
        for step in range(1, cores):
            for index in range(CHUNKS):
                forward(step, index).wait_recv()
        ke_v[...] = dot(xe[...], w_v[1]).astype(BF16)
        edge_valid = (
            lax.broadcasted_iota(jnp.int32, (rows, part), 0).astype(F32) < aux_e[heads, 0]
        )
        ve_v[...] = jnp.where(edge_valid, dot(xe[...], w_v[2]), 0.0).astype(BF16)
        for head in range(heads):
            span = slice(head * size, (head + 1) * size)
            t = dot_t(q_v[:, span], ke_v[:, span]) * half_scale + aux_e[pl.ds(head, 1), :]
            weight = jnp.where(below, 0.0, silu_from_half(t)).astype(BF16)
            value = (acc[:, span] + dot(weight, ve_v[:, span])) * out_scale
            out_ref[:, span] = jnp.where(valid[:, span], value, 0.0).astype(BF16)
        for step in range(1, cores):
            for index in range(CHUNKS):
                forward(step, index).wait_send()

    peers(lambda step: partial_copy(step).wait_recv())
    if unroll:
        summed = p_recv[pl.ds(0, tile), :]
        for index in range(1, n):
            summed = summed + p_recv[pl.ds(index * tile, tile), :]
    else:
        summed = lax.fori_loop(
            0,
            n,
            lambda i, s: s + p_recv[pl.ds(pl.multiple_of(i * tile, tile), tile), :],
            jnp.zeros((tile, p_recv.shape[1]), F32),
        )
    group_width = group_heads * size
    for index in range(fold):
        cand_out_ref[:, index * group_width : (index + 1) * group_width] = summed[
            index * cands : (index + 1) * cands, :
        ].astype(BF16)

    peers(lambda step: query_copy(step).wait_send())
    peers(lambda step: partial_copy(step).wait_send())

    @pl.when(me < n - 1)
    def _():
        aux_copy.wait_send()
        for index in range(CHUNKS):
            edge_copy(index).wait_send()


def local(n, cores, hist_x, cand_x, w_qkv, rab_table, hist_len, hist_bucket, cand_owner):
    rows, width = hist_x.shape
    part = w_qkv.shape[2]
    heads = rab_table.shape[1]
    size = part // heads
    cands = cand_x.shape[0]
    slot = cands * heads
    fold = max(1, 8 // cands)
    tile = fold * cands
    dma = pltpu.SemaphoreType.DMA
    vmem = pl.BlockSpec(memory_space=pltpu.VMEM)
    hbm = pl.BlockSpec(memory_space=pltpu.HBM)
    return pl.pallas_call(
        functools.partial(kernel, n, cores, heads),
        out_shape=(
            jax.ShapeDtypeStruct((rows, part), BF16),
            jax.ShapeDtypeStruct((cands, part), BF16),
        ),
        in_specs=[hbm] * 7,
        out_specs=(vmem, vmem),
        scratch_shapes=[
            pltpu.VMEM(cand_x.shape, BF16),
            pltpu.VMEM(rab_table.shape[::-1], F32),
            pltpu.SMEM(hist_len.shape, jnp.int32),
            pltpu.VMEM((1, rows), jnp.int32),
            pltpu.VMEM((1, cands * n), jnp.int32),
            pltpu.VMEM((rows, width), BF16),
            pltpu.VMEM(w_qkv.shape, BF16),
            pltpu.VMEM((rows, part), BF16),
            pltpu.VMEM((rows, part), BF16),
            pltpu.VMEM((rows, part), BF16),
            pltpu.VMEM((rows, width), BF16),
            pltpu.VMEM((rows, part), BF16),
            pltpu.VMEM((rows, part), BF16),
            pltpu.VMEM((rows, part), F32),
            pltpu.VMEM((8, rows), F32),
            pltpu.VMEM((8, rows), F32),
            pltpu.VMEM((slot, width), F32),
            pltpu.VMEM((slot, size), BF16),
            pltpu.VMEM((n * slot, size), BF16),
            pltpu.VMEM((n * tile, part // fold), F32),
            pltpu.VMEM((n * tile, part // fold), F32),
            dma((9,)),
            dma((n,)),
            dma((n,)),
            dma((n,)),
            dma((n,)),
            dma((CHUNKS,)),
            dma((CHUNKS,)),
            dma,
            dma,
            dma((max(cores - 1, 1), CHUNKS)),
            dma((max(cores - 1, 1), CHUNKS)),
        ],
        compiler_params=pltpu.CompilerParams(
            collective_id=0,
            has_side_effects=True,
            vmem_limit_bytes=VMEM_LIMIT,
        ),
    )(
        hist_x,
        w_qkv,
        cand_x,
        rab_table.T,
        hist_len,
        hist_bucket.reshape(1, rows),
        cand_owner.reshape(1, cands * n),
    )


def solution(mesh):
    placed = (
        P(("groups", "ctx"), None),
        P(("groups", "ctx"), None),
        P(None, None, "head"),
        P(None, "head"),
        P(("groups", "ctx")),
        P(("groups", "ctx")),
        P("groups"),
    )
    return jax.shard_map(
        functools.partial(local, mesh.shape["ctx"], mesh.shape["head"]),
        mesh=mesh,
        in_specs=placed,
        out_specs=(P(("groups", "ctx"), "head"), P(("groups", "ctx"), "head")),
        check_vma=False,
    )
```

```python
import functools

import jax
import jax.numpy as jnp
from jax import lax
from jax.experimental import pallas as pl
from jax.experimental.pallas import tpu as pltpu
from jax.sharding import PartitionSpec as P

WINDOW = 256
CHUNKS = 2
VMEM_LIMIT = 48 * 1024 * 1024
MESH = pl.DeviceIdType.MESH
F32 = jnp.float32
BF16 = jnp.bfloat16


def dot(a, b):
    return jnp.dot(a, b, preferred_element_type=F32)


def dot_t(a, b):
    return lax.dot_general(a, b, (((1,), (1,)), ((), ())), preferred_element_type=F32)


def silu_from_half(t):
    return t + t * jnp.tanh(t)


def kernel(
    n,
    cores,
    heads,
    x_hbm,
    w_hbm,
    cand_hbm,
    table_hbm,
    bucket_hbm,
    owner_hbm,
    len_hbm,
    out_ref,
    cand_out_ref,
    cand_ref,
    table_ref,
    len_ref,
    bucket_ref,
    owner_ref,
    x_v,
    w_v,
    q_v,
    k_v,
    v_v,
    xe,
    acc,
    aux,
    aux_e,
    cand_rows,
    q_send,
    q_recv,
    p_send,
    p_recv,
    load_sem,
    qs_sem,
    qr_sem,
    ps_sem,
    pr_sem,
    es_sem,
    er_sem,
    as_sem,
    ar_sem,
    fs_sem,
    fr_sem,
):
    group = lax.axis_index("groups")
    me = lax.axis_index("ctx")
    core = lax.axis_index("head")
    rows, width = x_v.shape
    part = q_v.shape[1]
    size = part // heads
    half_scale = 0.5 * size ** (-0.5)
    cands = cand_ref.shape[0]
    total = cands * n
    slot = cands * heads
    fold = max(1, 8 // cands)
    unroll = n <= 16

    def peers(body):
        if unroll:
            for step in range(1, n):
                body(step)
        else:
            lax.fori_loop(1, n, lambda step, carry: (body(step), carry)[1], 0)

    pairs = [
        (cand_hbm, cand_ref),
        (len_hbm, len_ref),
        (bucket_hbm, bucket_ref),
        (table_hbm, table_ref),
        (owner_hbm, owner_ref),
        (w_hbm.at[0], w_v.at[0]),
        (x_hbm, x_v),
        (w_hbm.at[1], w_v.at[1]),
        (w_hbm.at[2], w_v.at[2]),
    ]
    loads = [
        pltpu.make_async_copy(source, target, load_sem.at[index])
        for index, (source, target) in enumerate(pairs)
    ]
    for load in loads:
        load.start()

    barrier = pltpu.get_barrier_semaphore()

    def greet(step):
        pl.semaphore_signal(
            barrier,
            inc=1,
            device_id=(group, lax.rem(me + step, n), core),
            device_id_type=MESH,
        )

    peers(greet)
    for step in range(1, cores):
        pl.semaphore_signal(
            barrier,
            inc=1,
            device_id=(group, me, lax.rem(core + step, cores)),
            device_id_type=MESH,
        )

    for load in loads[:5]:
        load.wait()

    length = len_ref[0, 0]
    buckets = table_ref.shape[1]
    hot = (
        lax.broadcasted_iota(jnp.int32, (buckets, rows), 0) == bucket_ref[...]
    ).astype(F32)
    bias = lax.dot_general(
        table_ref[...].astype(BF16),
        hot.astype(BF16),
        (((1,), (0,)), ((), ())),
        preferred_element_type=F32,
    )
    aux[...] = jnp.full(aux.shape, length.astype(F32), F32)
    aux[pl.ds(0, heads), :] = 0.5 * bias

    for head in range(heads):
        cand_rows[pl.ds(head * cands, cands), :] = cand_ref[...].astype(F32)
    loads[5].wait()
    own = dot(cand_rows[...].astype(BF16), w_v[0])
    row_head = lax.broadcasted_iota(jnp.int32, (slot, size), 0) // cands
    picked = own[:, 0:size]
    for head in range(1, heads):
        picked = jnp.where(row_head == head, own[:, head * size : (head + 1) * size], picked)
    q_send[...] = picked.astype(BF16)
    own_slot = pl.ds(pl.multiple_of(me * slot, slot), slot)
    q_recv[own_slot, :] = picked.astype(BF16)

    loads[6].wait()
    loads[7].wait()
    k_v[...] = dot(x_v[...], w_v[1]).astype(BF16)
    loads[8].wait()
    valid = lax.broadcasted_iota(jnp.int32, (rows, part), 0) < length
    v_v[...] = jnp.where(valid, dot(x_v[...], w_v[2]), 0.0).astype(BF16)

    pl.semaphore_wait(barrier, n - 1 + cores - 1)

    def query_copy(step):
        return pltpu.make_async_remote_copy(
            src_ref=q_send,
            dst_ref=q_recv.at[own_slot, :],
            send_sem=qs_sem.at[step],
            recv_sem=qr_sem.at[step],
            device_id=(group, lax.rem(me + step, n), core),
            device_id_type=MESH,
        )

    peers(lambda step: query_copy(step).start())

    chunk = rows // (cores * CHUNKS)

    def rows_of(owner_core, index):
        first = owner_core * (chunk * CHUNKS) + index * chunk
        return pl.ds(pl.multiple_of(first, chunk), chunk)

    def edge_copy(index):
        return pltpu.make_async_remote_copy(
            src_ref=x_hbm.at[rows_of(core, index), :],
            dst_ref=xe.at[rows_of(core, index), :],
            send_sem=es_sem.at[index],
            recv_sem=er_sem.at[index],
            device_id=(group, lax.rem(me + 1, n), core),
            device_id_type=MESH,
        )

    aux_copy = pltpu.make_async_remote_copy(
        src_ref=aux,
        dst_ref=aux_e,
        send_sem=as_sem,
        recv_sem=ar_sem,
        device_id=(group, lax.rem(me + 1, n), core),
        device_id_type=MESH,
    )

    def forward(step, index):
        return pltpu.make_async_remote_copy(
            src_ref=xe.at[rows_of(core, index), :],
            dst_ref=xe.at[rows_of(core, index), :],
            send_sem=fs_sem.at[step - 1, index],
            recv_sem=fr_sem.at[step - 1, index],
            device_id=(group, me, lax.rem(core + step, cores)),
            device_id_type=MESH,
        )

    @pl.when(me < n - 1)
    def _():
        aux_copy.start()
        for index in range(CHUNKS):
            edge_copy(index).start()

    group_heads = heads // fold
    out_rows = n * fold * cands
    tall = lax.broadcasted_iota(jnp.int32, (out_rows, total), 0)
    place = (tall // (fold * cands)) * cands + lax.rem(tall, cands)
    sits = (owner_ref[...] == place).astype(F32).astype(BF16)
    lane = lax.broadcasted_iota(jnp.int32, (total, n * slot), 1)
    source = (lane // slot) * cands + lax.rem(lane, cands)
    spread = (lax.broadcasted_iota(jnp.int32, (total, n * slot), 0) == source).astype(F32)
    chosen = dot(sits, spread.astype(BF16))
    lane_head = lax.rem(
        lax.broadcasted_iota(jnp.int32, (out_rows, n * slot), 1) // cands, heads
    )
    row_fold = lax.rem(
        lax.broadcasted_iota(jnp.int32, (out_rows, n * slot), 0) // cands, fold
    )
    peers(lambda step: query_copy(step).wait_recv())
    norm = (rows * n) ** (-0.5)

    def folded(parts, shape):
        fold_of = lax.rem(lax.broadcasted_iota(jnp.int32, shape, 0) // cands, fold)
        value = parts[0]
        for index in range(1, fold):
            value = jnp.where(fold_of == index, parts[index], value)
        return value

    for column in range(group_heads):
        select = jnp.where(lane_head == row_fold * group_heads + column, chosen, 0.0)
        query = dot(select.astype(BF16), q_recv[...]).astype(BF16)
        heads_here = [f * group_heads + column for f in range(fold)]
        spans = [slice(h * size, (h + 1) * size) for h in heads_here]
        t = folded(
            [
                dot_t(query, k_v[:, span]) * half_scale + aux[pl.ds(h, 1), :]
                for h, span in zip(heads_here, spans)
            ],
            (out_rows, rows),
        )
        weight = silu_from_half(t).astype(BF16)
        p_send[:, column * size : (column + 1) * size] = norm * folded(
            [dot(weight, v_v[:, span]) for span in spans], (out_rows, size)
        )
    tile = fold * cands
    own_tile = pl.ds(pl.multiple_of(me * tile, tile), tile)

    def partial_copy(step):
        to = lax.rem(me + step, n)
        return pltpu.make_async_remote_copy(
            src_ref=p_send.at[pl.ds(pl.multiple_of(to * tile, tile), tile), :],
            dst_ref=p_recv.at[own_tile, :],
            send_sem=ps_sem.at[step],
            recv_sem=pr_sem.at[step],
            device_id=(group, to, core),
            device_id_type=MESH,
        )

    peers(lambda step: partial_copy(step).start())
    p_recv[own_tile, :] = p_send[own_tile, :]

    q_v[...] = dot(x_v[...], w_v[0]).astype(BF16)
    below = lax.broadcasted_iota(jnp.int32, (rows, rows), 0) >= lax.broadcasted_iota(
        jnp.int32, (rows, rows), 1
    )
    for head in range(heads):
        span = slice(head * size, (head + 1) * size)
        t = dot_t(q_v[:, span], k_v[:, span]) * half_scale + aux[pl.ds(head, 1), :]
        weight = jnp.where(below, silu_from_half(t), 0.0).astype(BF16)
        acc[:, span] = dot(weight, v_v[:, span])

    out_scale = WINDOW ** (-0.5)

    @pl.when(me == 0)
    def _():
        out_ref[...] = jnp.where(valid, acc[...] * out_scale, 0.0).astype(BF16)

    @pl.when(me > 0)
    def _():
        for index in range(CHUNKS):
            edge_copy(index).wait_recv()
            for step in range(1, cores):
                forward(step, index).start()
        aux_copy.wait_recv()
        half = rows // cores
        for step in range(cores):
            if step > 0:
                for index in range(CHUNKS):
                    forward(step, index).wait_recv()
            first = pl.multiple_of(lax.rem(core - step + cores, cores) * half, half)
            piece = pl.ds(first, half)
            edge_x = xe[piece, :]
            edge_keys = dot(edge_x, w_v[1]).astype(BF16)
            place = first + lax.broadcasted_iota(jnp.int32, (half, part), 0)
            edge_values = jnp.where(
                place.astype(F32) < aux_e[heads, 0], dot(edge_x, w_v[2]), 0.0
            ).astype(BF16)
            ahead = first + lax.broadcasted_iota(
                jnp.int32, (rows, half), 1
            ) > lax.broadcasted_iota(jnp.int32, (rows, half), 0)
            for head in range(heads):
                span = slice(head * size, (head + 1) * size)
                t = (
                    dot_t(q_v[:, span], edge_keys[:, span]) * half_scale
                    + aux_e[pl.ds(head, 1), piece]
                )
                weight = jnp.where(ahead, silu_from_half(t), 0.0).astype(BF16)
                value = acc[:, span] + dot(weight, edge_values[:, span])
                if step < cores - 1:
                    acc[:, span] = value
                else:
                    out_ref[:, span] = jnp.where(
                        valid[:, span], value * out_scale, 0.0
                    ).astype(BF16)
        for step in range(1, cores):
            for index in range(CHUNKS):
                forward(step, index).wait_send()

    peers(lambda step: partial_copy(step).wait_recv())
    if unroll:
        summed = p_recv[pl.ds(0, tile), :]
        for index in range(1, n):
            summed = summed + p_recv[pl.ds(index * tile, tile), :]
    else:
        summed = lax.fori_loop(
            0,
            n,
            lambda i, s: s + p_recv[pl.ds(pl.multiple_of(i * tile, tile), tile), :],
            jnp.zeros((tile, p_recv.shape[1]), F32),
        )
    group_width = group_heads * size
    for index in range(fold):
        cand_out_ref[:, index * group_width : (index + 1) * group_width] = summed[
            index * cands : (index + 1) * cands, :
        ].astype(BF16)

    peers(lambda step: query_copy(step).wait_send())
    peers(lambda step: partial_copy(step).wait_send())

    @pl.when(me < n - 1)
    def _():
        aux_copy.wait_send()
        for index in range(CHUNKS):
            edge_copy(index).wait_send()


def local(n, cores, hist_x, cand_x, w_qkv, rab_table, hist_len, hist_bucket, cand_owner):
    rows, width = hist_x.shape
    part = w_qkv.shape[2]
    heads = rab_table.shape[1]
    size = part // heads
    cands = cand_x.shape[0]
    slot = cands * heads
    fold = max(1, 8 // cands)
    tile = fold * cands
    dma = pltpu.SemaphoreType.DMA
    vmem = pl.BlockSpec(memory_space=pltpu.VMEM)
    hbm = pl.BlockSpec(memory_space=pltpu.HBM)
    return pl.pallas_call(
        functools.partial(kernel, n, cores, heads),
        out_shape=(
            pltpu.VMEM((rows, part), BF16),
            pltpu.VMEM((cands, part), BF16),
        ),
        in_specs=[hbm] * 7,
        out_specs=(vmem, vmem),
        scratch_shapes=[
            pltpu.VMEM(cand_x.shape, BF16),
            pltpu.VMEM(rab_table.shape[::-1], F32),
            pltpu.VMEM((1, 1), jnp.int32),
            pltpu.VMEM((1, rows), jnp.int32),
            pltpu.VMEM((1, cands * n), jnp.int32),
            pltpu.VMEM((rows, width), BF16),
            pltpu.VMEM(w_qkv.shape, BF16),
            pltpu.VMEM((rows, part), BF16),
            pltpu.VMEM((rows, part), BF16),
            pltpu.VMEM((rows, part), BF16),
            pltpu.VMEM((rows, width), BF16),
            pltpu.VMEM((rows, part), F32),
            pltpu.VMEM((8, rows), F32),
            pltpu.VMEM((8, rows), F32),
            pltpu.VMEM((slot, width), F32),
            pltpu.VMEM((slot, size), BF16),
            pltpu.VMEM((n * slot, size), BF16),
            pltpu.VMEM((n * tile, part // fold), F32),
            pltpu.VMEM((n * tile, part // fold), F32),
            dma((9,)),
            dma((n,)),
            dma((n,)),
            dma((n,)),
            dma((n,)),
            dma((CHUNKS,)),
            dma((CHUNKS,)),
            dma,
            dma,
            dma((max(cores - 1, 1), CHUNKS)),
            dma((max(cores - 1, 1), CHUNKS)),
        ],
        compiler_params=pltpu.CompilerParams(
            collective_id=0,
            has_side_effects=True,
            vmem_limit_bytes=VMEM_LIMIT,
        ),
    )(
        *(
            pltpu.with_memory_space_constraint(operand, pltpu.HBM)
            for operand in (
                hist_x,
                w_qkv,
                cand_x,
                rab_table.T,
                hist_bucket.reshape(1, rows),
                cand_owner.reshape(1, cands * n),
            )
        ),
        hist_len.reshape(1, 1),
    )


def solution(mesh):
    placed = (
        P(("groups", "ctx"), None),
        P(("groups", "ctx"), None),
        P(None, None, "head"),
        P(None, "head"),
        P(("groups", "ctx")),
        P(("groups", "ctx")),
        P("groups"),
    )
    return jax.shard_map(
        functools.partial(local, mesh.shape["ctx"], mesh.shape["head"]),
        mesh=mesh,
        in_specs=placed,
        out_specs=(P(("groups", "ctx"), "head"), P(("groups", "ctx"), "head")),
        check_vma=False,
    )
```

```python
import functools

import jax
import jax.numpy as jnp
from jax import lax
from jax.experimental import pallas as pl
from jax.experimental.pallas import tpu as pltpu
from jax.sharding import PartitionSpec as P

WINDOW = 256
CHUNKS = 2
VMEM_LIMIT = 48 * 1024 * 1024
MESH = pl.DeviceIdType.MESH
F32 = jnp.float32
BF16 = jnp.bfloat16


def dot(a, b):
    return jnp.dot(a, b, preferred_element_type=F32)


def dot_t(a, b):
    return lax.dot_general(a, b, (((1,), (1,)), ((), ())), preferred_element_type=F32)


def silu_from_half(t):
    return t + t * jnp.tanh(t)


def kernel(
    n,
    cores,
    heads,
    x_hbm,
    w_hbm,
    cand_hbm,
    table_hbm,
    bucket_hbm,
    owner_hbm,
    len_hbm,
    out_ref,
    cand_out_ref,
    cand_ref,
    table_ref,
    len_ref,
    bucket_ref,
    owner_ref,
    x_v,
    w_v,
    q_v,
    k_v,
    v_v,
    xe,
    acc,
    aux,
    aux_e,
    cand_rows,
    q_send,
    q_recv,
    p_send,
    p_recv,
    load_sem,
    qs_sem,
    qr_sem,
    ps_sem,
    pr_sem,
    es_sem,
    er_sem,
    as_sem,
    ar_sem,
    fs_sem,
    fr_sem,
):
    group = lax.axis_index("groups")
    me = lax.axis_index("ctx")
    core = lax.axis_index("head")
    rows, width = x_v.shape
    part = q_v.shape[1]
    size = part // heads
    half_scale = 0.5 * size ** (-0.5)
    cands = cand_ref.shape[0]
    total = cands * n
    slot = cands * heads
    fold = max(1, 8 // cands)
    unroll = n <= 16

    def peers(body):
        if unroll:
            for step in sorted(range(1, n), key=lambda s: -abs(2 * s - n)):
                body(step)
        else:
            lax.fori_loop(1, n, lambda step, carry: (body(step), carry)[1], 0)

    barrier = pltpu.get_barrier_semaphore()

    def greet(step):
        pl.semaphore_signal(
            barrier,
            inc=1,
            device_id=(group, lax.rem(me + step, n), core),
            device_id_type=MESH,
        )

    peers(greet)
    for step in range(1, cores):
        pl.semaphore_signal(
            barrier,
            inc=1,
            device_id=(group, me, lax.rem(core + step, cores)),
            device_id_type=MESH,
        )

    pairs = [
        (cand_hbm, cand_ref),
        (len_hbm, len_ref),
        (bucket_hbm, bucket_ref),
        (table_hbm, table_ref),
        (owner_hbm, owner_ref),
        (w_hbm.at[0], w_v.at[0]),
        (x_hbm, x_v),
        (w_hbm.at[1], w_v.at[1]),
        (w_hbm.at[2], w_v.at[2]),
    ]
    loads = [
        pltpu.make_async_copy(source, target, load_sem.at[index])
        for index, (source, target) in enumerate(pairs)
    ]
    for load in loads:
        load.start()

    for load in loads[:5]:
        load.wait()

    length = len_ref[0, 0]
    buckets = table_ref.shape[1]
    hot = (
        lax.broadcasted_iota(jnp.int32, (buckets, rows), 0) == bucket_ref[...]
    ).astype(F32)
    bias = lax.dot_general(
        table_ref[...].astype(BF16),
        hot.astype(BF16),
        (((1,), (0,)), ((), ())),
        preferred_element_type=F32,
    )
    aux[...] = jnp.full(aux.shape, length.astype(F32), F32)
    aux[pl.ds(0, heads), :] = 0.5 * bias

    for head in range(heads):
        cand_rows[pl.ds(head * cands, cands), :] = cand_ref[...].astype(F32)
    loads[5].wait()
    own = dot(cand_rows[...].astype(BF16), w_v[0])
    row_head = lax.broadcasted_iota(jnp.int32, (slot, size), 0) // cands
    picked = own[:, 0:size]
    for head in range(1, heads):
        picked = jnp.where(row_head == head, own[:, head * size : (head + 1) * size], picked)
    q_send[...] = picked.astype(BF16)
    own_slot = pl.ds(pl.multiple_of(me * slot, slot), slot)
    q_recv[own_slot, :] = picked.astype(BF16)

    loads[6].wait()
    loads[7].wait()
    k_v[...] = dot(x_v[...], w_v[1]).astype(BF16)
    loads[8].wait()
    valid = lax.broadcasted_iota(jnp.int32, (rows, part), 0) < length
    v_v[...] = jnp.where(valid, dot(x_v[...], w_v[2]), 0.0).astype(BF16)

    pl.semaphore_wait(barrier, n - 1 + cores - 1)

    def query_copy(step):
        return pltpu.make_async_remote_copy(
            src_ref=q_send,
            dst_ref=q_recv.at[own_slot, :],
            send_sem=qs_sem.at[step],
            recv_sem=qr_sem.at[step],
            device_id=(group, lax.rem(me + step, n), core),
            device_id_type=MESH,
        )

    peers(lambda step: query_copy(step).start())

    chunk = rows // (cores * CHUNKS)

    def rows_of(owner_core, index):
        first = owner_core * (chunk * CHUNKS) + index * chunk
        return pl.ds(pl.multiple_of(first, chunk), chunk)

    def edge_copy(index):
        return pltpu.make_async_remote_copy(
            src_ref=x_hbm.at[rows_of(core, index), :],
            dst_ref=xe.at[rows_of(core, index), :],
            send_sem=es_sem.at[index],
            recv_sem=er_sem.at[index],
            device_id=(group, lax.rem(me + 1, n), core),
            device_id_type=MESH,
        )

    aux_copy = pltpu.make_async_remote_copy(
        src_ref=aux,
        dst_ref=aux_e,
        send_sem=as_sem,
        recv_sem=ar_sem,
        device_id=(group, lax.rem(me + 1, n), core),
        device_id_type=MESH,
    )

    def forward(step, index):
        return pltpu.make_async_remote_copy(
            src_ref=xe.at[rows_of(core, index), :],
            dst_ref=xe.at[rows_of(core, index), :],
            send_sem=fs_sem.at[step - 1, index],
            recv_sem=fr_sem.at[step - 1, index],
            device_id=(group, me, lax.rem(core + step, cores)),
            device_id_type=MESH,
        )

    @pl.when(me < n - 1)
    def _():
        aux_copy.start()
        for index in range(CHUNKS):
            edge_copy(index).start()

    group_heads = heads // fold
    out_rows = n * fold * cands
    tall = lax.broadcasted_iota(jnp.int32, (out_rows, total), 0)
    place = (tall // (fold * cands)) * cands + lax.rem(tall, cands)
    sits = (owner_ref[...] == place).astype(F32).astype(BF16)
    lane = lax.broadcasted_iota(jnp.int32, (total, n * slot), 1)
    source = (lane // slot) * cands + lax.rem(lane, cands)
    spread = (lax.broadcasted_iota(jnp.int32, (total, n * slot), 0) == source).astype(F32)
    chosen = dot(sits, spread.astype(BF16))
    lane_head = lax.rem(
        lax.broadcasted_iota(jnp.int32, (out_rows, n * slot), 1) // cands, heads
    )
    row_fold = lax.rem(
        lax.broadcasted_iota(jnp.int32, (out_rows, n * slot), 0) // cands, fold
    )
    peers(lambda step: query_copy(step).wait_recv())
    norm = (rows * n) ** (-0.5)

    def folded(parts, shape):
        fold_of = lax.rem(lax.broadcasted_iota(jnp.int32, shape, 0) // cands, fold)
        value = parts[0]
        for index in range(1, fold):
            value = jnp.where(fold_of == index, parts[index], value)
        return value

    for column in range(group_heads):
        select = jnp.where(lane_head == row_fold * group_heads + column, chosen, 0.0)
        query = dot(select.astype(BF16), q_recv[...]).astype(BF16)
        heads_here = [f * group_heads + column for f in range(fold)]
        spans = [slice(h * size, (h + 1) * size) for h in heads_here]
        t = folded(
            [
                dot_t(query, k_v[:, span]) * half_scale + aux[pl.ds(h, 1), :]
                for h, span in zip(heads_here, spans)
            ],
            (out_rows, rows),
        )
        weight = silu_from_half(t).astype(BF16)
        p_send[:, column * size : (column + 1) * size] = norm * folded(
            [dot(weight, v_v[:, span]) for span in spans], (out_rows, size)
        )
    tile = fold * cands
    own_tile = pl.ds(pl.multiple_of(me * tile, tile), tile)

    def partial_copy(step):
        to = lax.rem(me + step, n)
        return pltpu.make_async_remote_copy(
            src_ref=p_send.at[pl.ds(pl.multiple_of(to * tile, tile), tile), :],
            dst_ref=p_recv.at[own_tile, :],
            send_sem=ps_sem.at[step],
            recv_sem=pr_sem.at[step],
            device_id=(group, to, core),
            device_id_type=MESH,
        )

    peers(lambda step: partial_copy(step).start())
    p_recv[own_tile, :] = p_send[own_tile, :]

    q_v[...] = dot(x_v[...], w_v[0]).astype(BF16)
    below = lax.broadcasted_iota(jnp.int32, (rows, rows), 0) >= lax.broadcasted_iota(
        jnp.int32, (rows, rows), 1
    )
    for head in range(heads):
        span = slice(head * size, (head + 1) * size)
        t = dot_t(q_v[:, span], k_v[:, span]) * half_scale + aux[pl.ds(head, 1), :]
        weight = jnp.where(below, silu_from_half(t), 0.0).astype(BF16)
        acc[:, span] = dot(weight, v_v[:, span])

    out_scale = WINDOW ** (-0.5)

    @pl.when(me == 0)
    def _():
        out_ref[...] = jnp.where(valid, acc[...] * out_scale, 0.0).astype(BF16)

    @pl.when(me > 0)
    def _():
        for index in range(CHUNKS):
            edge_copy(index).wait_recv()
            for step in range(1, cores):
                forward(step, index).start()
        aux_copy.wait_recv()
        half = rows // cores
        for step in range(cores):
            if step > 0:
                for index in range(CHUNKS):
                    forward(step, index).wait_recv()
            first = pl.multiple_of(lax.rem(core - step + cores, cores) * half, half)
            piece = pl.ds(first, half)
            edge_x = xe[piece, :]
            edge_keys = dot(edge_x, w_v[1]).astype(BF16)
            place = first + lax.broadcasted_iota(jnp.int32, (half, part), 0)
            edge_values = jnp.where(
                place.astype(F32) < aux_e[heads, 0], dot(edge_x, w_v[2]), 0.0
            ).astype(BF16)
            ahead = first + lax.broadcasted_iota(
                jnp.int32, (rows, half), 1
            ) > lax.broadcasted_iota(jnp.int32, (rows, half), 0)
            for head in range(heads):
                span = slice(head * size, (head + 1) * size)
                t = (
                    dot_t(q_v[:, span], edge_keys[:, span]) * half_scale
                    + aux_e[pl.ds(head, 1), piece]
                )
                weight = jnp.where(ahead, silu_from_half(t), 0.0).astype(BF16)
                value = acc[:, span] + dot(weight, edge_values[:, span])
                if step < cores - 1:
                    acc[:, span] = value
                else:
                    out_ref[:, span] = jnp.where(
                        valid[:, span], value * out_scale, 0.0
                    ).astype(BF16)
        for step in range(1, cores):
            for index in range(CHUNKS):
                forward(step, index).wait_send()

    peers(lambda step: partial_copy(step).wait_recv())
    if unroll:
        summed = p_recv[pl.ds(0, tile), :]
        for index in range(1, n):
            summed = summed + p_recv[pl.ds(index * tile, tile), :]
    else:
        summed = lax.fori_loop(
            0,
            n,
            lambda i, s: s + p_recv[pl.ds(pl.multiple_of(i * tile, tile), tile), :],
            jnp.zeros((tile, p_recv.shape[1]), F32),
        )
    group_width = group_heads * size
    for index in range(fold):
        cand_out_ref[:, index * group_width : (index + 1) * group_width] = summed[
            index * cands : (index + 1) * cands, :
        ].astype(BF16)

    peers(lambda step: query_copy(step).wait_send())
    peers(lambda step: partial_copy(step).wait_send())

    @pl.when(me < n - 1)
    def _():
        aux_copy.wait_send()
        for index in range(CHUNKS):
            edge_copy(index).wait_send()


def local(n, cores, hist_x, cand_x, w_qkv, rab_table, hist_len, hist_bucket, cand_owner):
    rows, width = hist_x.shape
    part = w_qkv.shape[2]
    heads = rab_table.shape[1]
    size = part // heads
    cands = cand_x.shape[0]
    slot = cands * heads
    fold = max(1, 8 // cands)
    tile = fold * cands
    dma = pltpu.SemaphoreType.DMA
    vmem = pl.BlockSpec(memory_space=pltpu.VMEM)
    hbm = pl.BlockSpec(memory_space=pltpu.HBM)
    return pl.pallas_call(
        functools.partial(kernel, n, cores, heads),
        out_shape=(
            pltpu.VMEM((rows, part), BF16),
            pltpu.VMEM((cands, part), BF16),
        ),
        in_specs=[hbm] * 7,
        out_specs=(vmem, vmem),
        scratch_shapes=[
            pltpu.VMEM(cand_x.shape, BF16),
            pltpu.VMEM(rab_table.shape[::-1], F32),
            pltpu.VMEM((1, 1), jnp.int32),
            pltpu.VMEM((1, rows), jnp.int32),
            pltpu.VMEM((1, cands * n), jnp.int32),
            pltpu.VMEM((rows, width), BF16),
            pltpu.VMEM(w_qkv.shape, BF16),
            pltpu.VMEM((rows, part), BF16),
            pltpu.VMEM((rows, part), BF16),
            pltpu.VMEM((rows, part), BF16),
            pltpu.VMEM((rows, width), BF16),
            pltpu.VMEM((rows, part), F32),
            pltpu.VMEM((8, rows), F32),
            pltpu.VMEM((8, rows), F32),
            pltpu.VMEM((slot, width), F32),
            pltpu.VMEM((slot, size), BF16),
            pltpu.VMEM((n * slot, size), BF16),
            pltpu.VMEM((n * tile, part // fold), F32),
            pltpu.VMEM((n * tile, part // fold), F32),
            dma((9,)),
            dma((n,)),
            dma((n,)),
            dma((n,)),
            dma((n,)),
            dma((CHUNKS,)),
            dma((CHUNKS,)),
            dma,
            dma,
            dma((max(cores - 1, 1), CHUNKS)),
            dma((max(cores - 1, 1), CHUNKS)),
        ],
        compiler_params=pltpu.CompilerParams(
            collective_id=0,
            has_side_effects=True,
            vmem_limit_bytes=VMEM_LIMIT,
        ),
    )(
        *(
            pltpu.with_memory_space_constraint(operand, pltpu.HBM)
            for operand in (
                hist_x,
                w_qkv,
                cand_x,
                rab_table.T,
                hist_bucket.reshape(1, rows),
                cand_owner.reshape(1, cands * n),
            )
        ),
        hist_len.reshape(1, 1),
    )


def solution(mesh):
    placed = (
        P(("groups", "ctx"), None),
        P(("groups", "ctx"), None),
        P(None, None, "head"),
        P(None, "head"),
        P(("groups", "ctx")),
        P(("groups", "ctx")),
        P("groups"),
    )
    return jax.shard_map(
        functools.partial(local, mesh.shape["ctx"], mesh.shape["head"]),
        mesh=mesh,
        in_specs=placed,
        out_specs=(P(("groups", "ctx"), "head"), P(("groups", "ctx"), "head")),
        check_vma=False,
    )
```
